256 devices in a mesh: sec: 64 (over z, y, core), tile: 4 (over x).
Axes of the slice: x: 4, y: 4, z: 8, core: 2. Of those that a mesh axis runs over, the one named last changes fastest.
Arguments:
- patches: bfloat16 [384, 8, 8, 128, 128], P('sec', 'tile'), may hold values from -6 to 6
- pair_flags: int32 [384, 3], P('sec'), may hold values 0 or 1
- nodes: float32 [2, 384, 8, 8], P(None, 'sec', 'tile'), may hold values from -6 to 6
Outputs:
- relaxed: float32 [2, 384, 8, 8], P(None, 'sec', 'tile')
- measured: float32 [2, 384, 3, 8, 8], P(None, 'sec', None, 'tile')
The draws below stay inside these ranges and needn't reach their ends.
Inputs may be any that keep to these rules, and one draw needn't show every extreme that they name: `pair_flags`: flags of pairs whose partner lies past the last section are ignored.
All inputs are finite; a program needn't handle non-finite values. No bound on the sum of `pair_flags` on one device may be relied on, other than what follows from the above.
Results may differ from the reference program's by a relative error of at most 0.0081.
Values may be sent and summed in bfloat16 or wider, within the bound.
No kernel may reach another device: no remote copies, remote signals or barrier semaphores. Data moves between devices by JAX's collectives and lax.ppermute only.
A program may use at most 128 MiB of HBM per device.

```python
import math
import jax
import jax.numpy as jnp
from jax import lax

P_SIZE = 128
COLS = 8
OFFS = 3
SWEEPS = 8
SECTIONS = 384
ROWS = 8


def place_ends(drawn, rng, smallest, high):
    index_at = [jax.random.randint(jax.random.fold_in(rng, axis), (), 0, length) for axis, length in enumerate(drawn.shape)]
    longest = drawn.shape.index(max(drawn.shape))
    next_to = index_at[:longest] + [(index_at[longest] + 1) % drawn.shape[longest]] + index_at[longest + 1:]
    return drawn.at[tuple(index_at)].set(smallest).at[tuple(next_to)].set(high)


def steps_of(rng, shape, split, low, high):
    factor_of = 1.0
    for position, shards_of in split:
        heights = jax.random.uniform(jax.random.fold_in(jax.random.fold_in(rng, 6), position), (shards_of,), jnp.float32, low / len(split), high / len(split))
        factor_of = factor_of * jnp.repeat(jnp.exp(heights), shape[position] // shards_of).reshape((-1,) + (1,) * (len(shape) - 1 - position))
    return factor_of


def centred(own_key, dims, width, most, split=(), held_as=jnp.bfloat16):
    gain = steps_of(own_key, dims, split, -0.22, 0.18) if split else 1.0
    entries = jax.random.normal(own_key, dims, jnp.float32) * width * gain
    return jnp.minimum(jnp.maximum(entries, -most), most).astype(held_as)


def setup_inputs(seed: int = 0) -> dict:
    streams_of = jax.random.split(jax.random.key(seed), 4)
    patches = centred(streams_of[0], (SECTIONS, ROWS, COLS, P_SIZE, P_SIZE), 1.0, 6.0, ((0, 64), (1, 4)))
    pair_flags = place_ends((jax.random.randint(streams_of[1], (SECTIONS, OFFS), 0, 3) < 2).astype(jnp.int32), jax.random.fold_in(streams_of[1], 1), 0, 1)
    nodes = centred(streams_of[2], (2, SECTIONS, ROWS, COLS), 1.0, 6.0, ((1, 64), (2, 4)), jnp.float32)
    return {"patches": patches, "pair_flags": pair_flags, "nodes": nodes}


STEP_SIZE = 0.08
EPSILON = 1e-6


def transform_tables(length):
    index = jnp.arange(length, dtype=jnp.int32)
    phase = ((index[:, None] * index[None, :]) % length).astype(jnp.float32) * (2.0 * math.pi / length)
    cosine = jnp.cos(phase)
    sine = jnp.sin(phase)
    forward_first = jnp.concatenate([cosine, sine], axis=1).astype(jnp.bfloat16)
    forward_second = jnp.stack([jnp.stack([cosine, -sine], 1), jnp.stack([-sine, -cosine], 1)], 0).astype(jnp.bfloat16)
    inverse_first = jnp.stack([jnp.stack([cosine, sine], 1), jnp.stack([-sine, cosine], 1)], 0).astype(jnp.bfloat16)
    inverse_second = jnp.stack([cosine, -sine], 1).astype(jnp.bfloat16)
    shifts = jnp.where(index < length // 2, index, index - length).astype(jnp.float32)
    return forward_first, forward_second, inverse_first, inverse_second, shifts


def spectrum(block, tabs):
    length = block.shape[-1]
    half = jnp.einsum("...aj,jm->...am", block.astype(jnp.float32), tabs[0].astype(jnp.float32)).astype(jnp.bfloat16)
    half = half.reshape(half.shape[:-1] + (2, length))
    return jnp.einsum("rahj,...jhk->...rak", tabs[1].astype(jnp.float32), half.astype(jnp.float32)).astype(jnp.bfloat16)


def measure(first_spec, second_spec, weight, tabs):
    length = first_spec.shape[-1]
    left = first_spec.astype(jnp.float32)
    right = second_spec.astype(jnp.float32)
    real = left[..., 0, :, :] * right[..., 0, :, :] + left[..., 1, :, :] * right[..., 1, :, :]
    imag = left[..., 0, :, :] * right[..., 1, :, :] - left[..., 1, :, :] * right[..., 0, :, :]
    cross = jnp.stack([real, imag], axis=-3).astype(jnp.bfloat16)
    back = jnp.einsum("...qaj,qjrk->...rak", cross.astype(jnp.float32), tabs[2].astype(jnp.float32)).astype(jnp.bfloat16)
    corr = jnp.einsum("arj,...rjk->...ak", tabs[3].astype(jnp.float32), back.astype(jnp.float32)) * (1.0 / float(length) ** 3)
    power = corr * corr
    total = jnp.mean(power, axis=(-2, -1)) + EPSILON
    along_rows = jnp.mean(power * tabs[4][:, None], axis=(-2, -1))
    along_cols = jnp.mean(power * tabs[4][None, :], axis=(-2, -1))
    return jnp.stack([along_rows / total, along_cols / total], 0) * weight


def plane_force(u):
    rows = u.shape[2]
    cols = u.shape[3]
    row_place = jnp.arange(rows, dtype=jnp.int32)
    col_place = jnp.arange(cols, dtype=jnp.int32)
    has_up = (row_place > 0).astype(jnp.float32)[:, None]
    has_down = (row_place < rows - 1).astype(jnp.float32)[:, None]
    has_left = (col_place > 0).astype(jnp.float32)[None, :]
    has_right = (col_place < cols - 1).astype(jnp.float32)[None, :]
    zero_row = jnp.zeros_like(u[:, :, :1])
    zero_col = jnp.zeros_like(u[..., :1])
    above = jnp.concatenate([zero_row, u[:, :, :-1]], axis=2)
    below = jnp.concatenate([u[:, :, 1:], zero_row], axis=2)
    left = jnp.concatenate([zero_col, u[..., :-1]], axis=3)
    right = jnp.concatenate([u[..., 1:], zero_col], axis=3)
    return has_up * (above - u) + has_down * (below - u) + has_left * (left - u) + has_right * (right - u)


def reference(patches, pair_flags, nodes):
    tabs = transform_tables(P_SIZE)
    spectra = lax.map(lambda block: spectrum(block, tabs), patches)
    sections = patches.shape[0]
    offsets = jnp.arange(1, OFFS + 1, dtype=jnp.int32)
    placed = jnp.arange(sections, dtype=jnp.int32)
    weights = pair_flags.astype(jnp.float32) * ((placed[:, None] + offsets[None, :]) < sections).astype(jnp.float32)

    def per_section(index):
        own = lax.dynamic_index_in_dim(spectra, index, 0, keepdims=False)
        results = []
        for step in range(OFFS):
            where = jnp.minimum(index + step + 1, sections - 1).astype(jnp.int32)
            other = lax.dynamic_index_in_dim(spectra, where, 0, keepdims=False)
            results.append(measure(own, other, weights[index, step], tabs))
        return jnp.stack(results, axis=1)

    measured = lax.map(per_section, placed)
    measured = jnp.transpose(measured, (1, 0, 2, 3, 4))
    u = nodes
    for sweep in range(SWEEPS):
        spring = jnp.zeros_like(u)
        for step in range(OFFS):
            offset = step + 1
            ahead = jnp.concatenate([u[:, offset:], jnp.zeros_like(u[:, :offset])], axis=1)
            resid = weights[None, :, step, None, None] * (ahead - u - measured[:, :, step])
            spring = spring + resid - jnp.concatenate([jnp.zeros_like(resid[:, :offset]), resid[:, :sections - offset]], axis=1)
        u = u + STEP_SIZE * (plane_force(u) + spring)
    return u, measured
```

```python
import functools

import jax
import jax.numpy as jnp
import ml_dtypes
import numpy as np
from jax import lax
from jax.experimental import pallas as pl
from jax.experimental.pallas import tpu as pltpu
from jax.sharding import PartitionSpec as P

SWEEPS = 8
STEP_SIZE = 0.08
EPSILON = 1e-06
LENGTH = 128
HALF = 64
LANES = 128
FULL = 80


def tables():
    index = np.arange(LENGTH)
    phase = (index[:, None] * index[None, :] % LENGTH) * (2.0 * np.pi / LENGTH)
    cosine, sine = np.cos(phase), np.sin(phase)
    shifts = np.where(index < HALF, index, index - LENGTH).astype(np.float64)
    rows = np.zeros((144, LENGTH))
    rows[:HALF] = cosine[:HALF]
    rows[HALF:LENGTH] = sine[:HALF]
    rows[LENGTH] = cosine[HALF]
    cols = np.block([[cosine, -sine], [-sine, -cosine]])
    back = np.block([[cosine, sine], [-sine, cosine]])
    basis = np.concatenate([2.0 * cosine[:, :HALF], -2.0 * sine[:, :HALF]], axis=1)
    basis[:, 0] = 1.0
    basis[:, HALF] = cosine[:, HALF]
    form = basis.T @ (shifts[:, None] * basis)
    cos_part = np.arange(LENGTH) <= HALF
    half_form = np.where(cos_part[None, :], form, 2.0 * form)
    weigh = np.zeros((FULL, LENGTH))
    weigh[: HALF + 1] = half_form[: HALF + 1]
    weigh = np.where(np.abs(weigh) < 1e-6, 0.0, weigh)
    return tuple(t.astype(ml_dtypes.bfloat16) for t in (rows, cols, back, weigh))


def dot(a, b):
    return lax.dot_general(a, b, (((1,), (0,)), ((), ())), preferred_element_type=jnp.float32)


def spectra(patches, rows_ref, cols_ref):
    part = dot(rows_ref[...], jnp.concatenate(patches, axis=1)).astype(jnp.bfloat16)
    stacked = []
    for s in range(len(patches)):
        lanes = slice(s * LANES, (s + 1) * LANES)
        stacked.append(jnp.concatenate([part[:HALF, lanes], part[HALF:LENGTH, lanes]], axis=1))
        stacked.append(
            jnp.concatenate([part[LENGTH:, lanes], jnp.zeros((16, LANES), jnp.bfloat16)], axis=1)
        )
    return dot(jnp.concatenate(stacked, axis=0), cols_ref[...]).astype(jnp.bfloat16)


def cross(a, b):
    a = a[:72].astype(jnp.float32)
    b = b[:72].astype(jnp.float32)
    ar, ai = a[:, :LANES], a[:, LANES:]
    br, bi = b[:, :LANES], b[:, LANES:]
    real = ar * br + ai * bi
    imag = ar * bi - ai * br
    top_real = real[:8] - imag[HALF:]
    top_imag = imag[:8] + real[HALF:]
    real = jnp.concatenate([top_real, real[8:HALF]], axis=0)
    imag = jnp.concatenate([top_imag, imag[8:HALF]], axis=0)
    return jnp.concatenate([real, imag], axis=1).astype(jnp.bfloat16)


def tile_sum(values):
    total = values[0:8]
    for v in range(1, HALF // 8):
        total = total + values[8 * v : 8 * v + 8]
    return total


def moments(pairs, back_ref, weigh_ref, places):
    count = len(pairs)
    back = dot(jnp.concatenate(pairs, axis=0), back_ref[...])
    reals = [back[HALF * n : HALF * n + HALF, :LANES] for n in range(count)]
    imags = [back[HALF * n : HALF * n + HALF, LANES:] for n in range(count)]
    stacked = jnp.concatenate(
        [jnp.concatenate([r, i], axis=0).astype(jnp.bfloat16) for r, i in zip(reals, imags)], axis=1
    )
    weighed = dot(weigh_ref[...], stacked)
    first = lax.broadcasted_iota(jnp.int32, (8, LANES), 0) == 0
    powers = [jnp.zeros((1, LANES), jnp.float32)] * 24
    alongs = list(powers)
    for n in range(count):
        real, imag = reals[n], imags[n]
        square = real * real + imag * imag
        power = 2.0 * tile_sum(square) - jnp.where(first, square[:8], 0.0)
        lanes = slice(n * LANES, (n + 1) * LANES)
        along = tile_sum(real * weighed[:HALF, lanes]) + imag[:8] * weighed[HALF:72, lanes]
        powers[places[n]] = jnp.sum(power, axis=0, keepdims=True)
        alongs[places[n]] = jnp.sum(along, axis=0, keepdims=True)
    power = jnp.concatenate(powers, axis=0)
    along = jnp.concatenate(alongs, axis=0)
    place = lax.broadcasted_iota(jnp.int32, (24, LANES), 1)
    shift = jnp.where(place < HALF, place, place - LENGTH).astype(jnp.float32)
    total = jnp.sum(power, axis=1, keepdims=True) * 2.0**-49 + EPSILON
    by_rows = jnp.sum(along, axis=1, keepdims=True) * 2.0**-56
    by_cols = jnp.sum(power * shift, axis=1, keepdims=True) * 2.0**-49
    return by_rows / total, by_cols / total


def put(acc_ref, node, values):
    lane = lax.broadcasted_iota(jnp.int32, (24, LANES), 1)
    acc_ref[...] = jnp.where(
        lane == node, values[0], jnp.where(lane == node + HALF, values[1], acc_ref[...])
    )


def own_kernel(patches_ref, rows_ref, cols_ref, back_ref, weigh_ref, acc_ref, kept_ref):
    node = pl.program_id(0)

    @pl.when(node == 0)
    def _():
        acc_ref[...] = jnp.zeros_like(acc_ref)

    spec = spectra([patches_ref[s, 0] for s in range(6)], rows_ref, cols_ref)
    specs = [spec[FULL * s : FULL * s + FULL] for s in range(6)]
    for s in range(3):
        kept_ref[0, s] = specs[3 + s]
    chosen = [(s, o) for o in (1, 2, 3) for s in range(6 - o)]
    pairs = [cross(specs[s], specs[s + o]) for s, o in chosen]
    put(acc_ref, node, moments(pairs, back_ref, weigh_ref, [8 * (o - 1) + s for s, o in chosen]))


def next_kernel(
    tile_ref, patches_ref, kept_ref, rows_ref, cols_ref, back_ref, weigh_ref,
    own_ref, weights_ref, nodes_ref, measured_ref, message_ref,
):
    node = pl.program_id(0)

    @pl.when(node == 0)
    def _():
        measured_ref[...] = own_ref[...]

    spec = spectra([patches_ref[s, 0] for s in range(3)], rows_ref, cols_ref)
    ahead = [spec[FULL * s : FULL * s + FULL] for s in range(3)]
    chosen = [(s, o) for o in (1, 2, 3) for s in range(6 - o, 6)]
    pairs = [cross(kept_ref[0, s - 3], ahead[s + o - 6]) for s, o in chosen]
    place = [8 * (o - 1) + s for s, o in chosen]
    row = lax.broadcasted_iota(jnp.int32, (24, LANES), 0)
    mine = functools.reduce(jnp.logical_or, [row == p for p in place])
    lane = lax.broadcasted_iota(jnp.int32, (24, LANES), 1)
    by_rows, by_cols = moments(pairs, back_ref, weigh_ref, place)
    old = measured_ref[...]
    new = jnp.where(mine & (lane == node), by_rows, old)
    measured_ref[...] = jnp.where(mine & (lane == node + HALF), by_cols, new)

    @pl.when(node == pl.num_programs(0) - 1)
    def _():
        measured = measured_ref[...] * weights_ref[...]
        measured_ref[...] = measured
        turn = tile_ref[0] * 16
        row = lax.broadcasted_iota(jnp.int32, (8, LANES), 0)
        zero = jnp.zeros((8, LANES), jnp.float32)
        low = jnp.zeros((16, LANES), jnp.float32)
        for o in (1, 2, 3):
            part = measured[8 * o - 8 : 8 * o]
            wide = jnp.concatenate([part, zero], axis=0)
            low = low - wide + pltpu.roll(wide, o, 0)
        lane = lax.broadcasted_iota(jnp.int32, (8, LANES), 1)
        flags = zero
        for o in (1, 2, 3):
            flags = jnp.where(lane == o - 1, weights_ref[8 * o - 8 : 8 * o], flags)
        message = jnp.concatenate([nodes_ref[...], flags, low], axis=0)
        message_ref[...] = pltpu.roll(message, turn, 1)


def relax_kernel(tile_ref, near_ref, low_ref, high_ref, out_ref, u_ref, w_ref, b_ref):
    u_ref[...] = jnp.zeros_like(u_ref)
    w_ref[...] = jnp.zeros_like(w_ref)
    b_ref[...] = jnp.zeros_like(b_ref)
    for trio, centre in ((low_ref, 1), (near_ref, 4), (high_ref, 7)):
        for part, by in ((0, 0), (1, -1), (2, 1)):
            row = 6 * (centre + by)
            u_ref[row : row + 6] = trio[part, 0:6]
            w_ref[row : row + 6] = trio[part, 8:14]
            b_ref[row : row + 9] += trio[part, 16:25]
    u = u_ref[...]
    flags = w_ref[...]
    lane = lax.broadcasted_iota(jnp.int32, u.shape, 1)
    weights = [
        jnp.sum(jnp.where(lane % 16 == o, flags, 0.0)[:, :HALF], axis=1, keepdims=True) * 0.25
        for o in range(3)
    ]
    weights = [jnp.broadcast_to(w, u.shape) for w in weights]
    pull = b_ref[...]
    col = lane % 8
    row = (lane // 8) % 8
    masks = [
        (m.astype(jnp.float32), by)
        for m, by in ((col > 0, 1), (col < 7, LANES - 1), (row > 0, 8), (row < 7, LANES - 8))
    ]
    degree = masks[0][0] + masks[1][0] + masks[2][0] + masks[3][0]
    for _ in range(SWEEPS):
        force = pull - degree * u
        for mask, by in masks:
            force = force + mask * pltpu.roll(u, by, 1)
        for o in (1, 2, 3):
            resid = weights[o - 1] * (pltpu.roll(u, u.shape[0] - o, 0) - u)
            force = force + resid - pltpu.roll(resid, o, 0)
        u = u + STEP_SIZE * force
    u_ref[...] = u
    turn = lax.rem(LANES - tile_ref[0] * 16, LANES)
    out_ref[...] = pltpu.roll(u_ref[24:32], turn, 1)


def shifted(value, axis, by):
    count = lax.axis_size(axis)
    pairs = [(i, i + by) for i in range(count) if 0 <= i + by < count]
    return lax.ppermute(value, axis, pairs)


def turned_by(value, axis, by):
    count = lax.axis_size(axis)
    return lax.ppermute(value, axis, [(i, (i + by) % count) for i in range(count)])


def shards(patches, pair_flags, nodes):
    local, rows_local, columns = patches.shape[:3]
    reach = pair_flags.shape[1]
    count = rows_local * columns
    flat = patches.reshape(local, count, LENGTH, LENGTH)
    tabs = tables()
    received = shifted(flat[:reach], "sec", -1)
    table_specs = [pl.BlockSpec(t.shape, lambda n: (0, 0)) for t in tabs]
    whole = pl.BlockSpec((24, LANES), lambda n: (0, 0))
    params = pltpu.CompilerParams(vmem_limit_bytes=48 * 1024 * 1024)
    own, kept = pl.pallas_call(
        own_kernel,
        grid=(count,),
        in_specs=[pl.BlockSpec((local, 1, LENGTH, LENGTH), lambda n: (0, n, 0, 0)), *table_specs],
        out_specs=[whole, pl.BlockSpec((1, 3, FULL, 2 * LANES), lambda n: (n, 0, 0, 0))],
        out_shape=[
            jax.ShapeDtypeStruct((24, LANES), jnp.float32),
            jax.ShapeDtypeStruct((count, 3, FULL, 2 * LANES), jnp.bfloat16),
        ],
        compiler_params=params,
        cost_estimate=pl.CostEstimate(flops=8_000_000_000, bytes_accessed=6_000_000, transcendentals=0),
        name="own_pairs",
    )(flat, *tabs)

    sections = lax.axis_size("sec") * local
    placed = lax.axis_index("sec") * local + jnp.arange(local, dtype=jnp.int32)
    offsets = jnp.arange(1, reach + 1, dtype=jnp.int32)
    weights = pair_flags.astype(jnp.float32) * (
        placed[:, None] + offsets[None, :] < sections
    ).astype(jnp.float32)
    weight_rows = jnp.broadcast_to(
        jnp.pad(weights.T, ((0, 0), (0, 2)))[:, :, None], (reach, 8, LANES)
    ).reshape(24, LANES)
    node_rows = jnp.pad(
        jnp.transpose(nodes, (1, 0, 2, 3)).reshape(local, 2, count), ((0, 2), (0, 0), (0, HALF - count))
    ).reshape(8, LANES)
    tile = lax.axis_index("tile").astype(jnp.int32).reshape(1)

    smem = pl.BlockSpec(memory_space=pltpu.SMEM)
    measured_rows, message = pl.pallas_call(
        next_kernel,
        grid=(count,),
        in_specs=[
            smem,
            pl.BlockSpec((reach, 1, LENGTH, LENGTH), lambda n: (0, n, 0, 0)),
            pl.BlockSpec((1, 3, FULL, 2 * LANES), lambda n: (n, 0, 0, 0)),
            *table_specs,
            whole,
            whole,
            pl.BlockSpec((8, LANES), lambda n: (0, 0)),
        ],
        out_specs=[whole, pl.BlockSpec((32, LANES), lambda n: (0, 0))],
        out_shape=[
            jax.ShapeDtypeStruct((24, LANES), jnp.float32),
            jax.ShapeDtypeStruct((32, LANES), jnp.float32),
        ],
        compiler_params=params,
        cost_estimate=pl.CostEstimate(flops=4_000_000_000, bytes_accessed=4_000_000, transcendentals=0),
        name="next_pairs",
    )(tile, received, kept, *tabs, own, weight_rows, node_rows)

    joined = message
    for by in range(1, lax.axis_size("tile")):
        joined = joined + turned_by(message, "tile", by)
    near = jnp.stack([joined, turned_by(joined, "sec", 1), turned_by(joined, "sec", -1)], axis=0)
    low = turned_by(near, "sec", 3)
    high = turned_by(near, "sec", -3)
    relaxed_rows = pl.pallas_call(
        relax_kernel,
        in_specs=[smem] + [pl.BlockSpec(memory_space=pltpu.VMEM)] * 3,
        out_specs=pl.BlockSpec(memory_space=pltpu.VMEM),
        out_shape=jax.ShapeDtypeStruct((8, LANES), jnp.float32),
        scratch_shapes=[pltpu.VMEM((64, LANES), jnp.float32)] * 3,
        name="relax",
    )(tile, near, low, high)

    measured = jnp.transpose(
        measured_rows.reshape(reach, 8, 2, HALF)[:, :local, :, :count], (2, 1, 0, 3)
    ).reshape(2, local, reach, rows_local, columns)
    relaxed = jnp.transpose(
        relaxed_rows.reshape(8, 2, HALF)[:local, :, :count], (1, 0, 2)
    ).reshape(2, local, rows_local, columns)
    return relaxed, measured


def solution(mesh):
    placed = (P("sec", "tile", None, None, None), P("sec", None), P(None, "sec", "tile", None))
    return jax.shard_map(
        shards,
        mesh=mesh,
        in_specs=placed,
        out_specs=(P(None, "sec", "tile", None), P(None, "sec", None, "tile", None)),
        check_vma=False,
    )
```

```python
import functools

import jax
import jax.numpy as jnp
import ml_dtypes
import numpy as np
from jax import lax
from jax.experimental import pallas as pl
from jax.experimental.pallas import tpu as pltpu
from jax.sharding import PartitionSpec as P

SWEEPS = 8
STEP_SIZE = 0.08
EPSILON = 1e-06
LENGTH = 128
HALF = 64
LANES = 128
OWN_NODES = 8
NEXT_NODES = 8
FULL = 80


def tables():
    index = np.arange(LENGTH)
    phase = (index[:, None] * index[None, :] % LENGTH) * (2.0 * np.pi / LENGTH)
    cosine, sine = np.cos(phase), np.sin(phase)
    shifts = np.where(index < HALF, index, index - LENGTH).astype(np.float64)
    rows = np.zeros((144, LENGTH))
    rows[:HALF] = cosine[:HALF]
    rows[HALF:LENGTH] = sine[:HALF]
    rows[LENGTH] = cosine[HALF]
    cols = np.block([[cosine, -sine], [-sine, -cosine]])
    back = np.block([[cosine, sine], [-sine, cosine]])
    basis = np.concatenate([2.0 * cosine[:, :HALF], -2.0 * sine[:, :HALF]], axis=1)
    basis[:, 0] = 1.0
    basis[:, HALF] = cosine[:, HALF]
    form = basis.T @ (shifts[:, None] * basis)
    cos_part = np.arange(LENGTH) <= HALF
    half_form = np.where(cos_part[None, :], form, 2.0 * form)
    weigh = np.zeros((FULL, LENGTH))
    weigh[: HALF + 1] = half_form[: HALF + 1]
    weigh = np.where(np.abs(weigh) < 1e-6, 0.0, weigh)
    return tuple(t.astype(ml_dtypes.bfloat16) for t in (rows, cols, back, weigh))


def dot(a, b):
    return lax.dot_general(a, b, (((1,), (0,)), ((), ())), preferred_element_type=jnp.float32)


def spectra(patches, rows_ref, cols_ref):
    part = dot(rows_ref[...], jnp.concatenate(patches, axis=1)).astype(jnp.bfloat16)
    stacked = []
    for s in range(len(patches)):
        lanes = slice(s * LANES, (s + 1) * LANES)
        stacked.append(jnp.concatenate([part[:HALF, lanes], part[HALF:LENGTH, lanes]], axis=1))
        stacked.append(
            jnp.concatenate([part[LENGTH:, lanes], jnp.zeros((16, LANES), jnp.bfloat16)], axis=1)
        )
    return dot(jnp.concatenate(stacked, axis=0), cols_ref[...]).astype(jnp.bfloat16)


def cross(a, b):
    a = a[:72].astype(jnp.float32)
    b = b[:72].astype(jnp.float32)
    ar, ai = a[:, :LANES], a[:, LANES:]
    br, bi = b[:, :LANES], b[:, LANES:]
    real = ar * br + ai * bi
    imag = ar * bi - ai * br
    top_real = real[:8] - imag[HALF:]
    top_imag = imag[:8] + real[HALF:]
    real = jnp.concatenate([top_real, real[8:HALF]], axis=0)
    imag = jnp.concatenate([top_imag, imag[8:HALF]], axis=0)
    return jnp.concatenate([real, imag], axis=1).astype(jnp.bfloat16)


def tile_sum(values):
    total = values[0:8]
    for v in range(1, HALF // 8):
        total = total + values[8 * v : 8 * v + 8]
    return total


def moments(pairs, back_ref, weigh_ref):
    count = len(pairs)
    back = dot(jnp.concatenate(pairs, axis=0), back_ref[...])
    reals = [back[HALF * n : HALF * n + HALF, :LANES] for n in range(count)]
    imags = [back[HALF * n : HALF * n + HALF, LANES:] for n in range(count)]
    stacked = jnp.concatenate(
        [jnp.concatenate([r, i], axis=0).astype(jnp.bfloat16) for r, i in zip(reals, imags)], axis=1
    )
    weighed = dot(weigh_ref[...], stacked)
    first = lax.broadcasted_iota(jnp.int32, (8, LANES), 0) == 0
    powers, alongs = [], []
    for n in range(count):
        real, imag = reals[n], imags[n]
        square = real * real + imag * imag
        power = 2.0 * tile_sum(square) - jnp.where(first, square[:8], 0.0)
        lanes = slice(n * LANES, (n + 1) * LANES)
        along = tile_sum(real * weighed[:HALF, lanes]) + imag[:8] * weighed[HALF:72, lanes]
        powers.append(jnp.sum(power, axis=0, keepdims=True))
        alongs.append(jnp.sum(along, axis=0, keepdims=True))
    return powers, alongs


def shifts_of(powers, alongs, places):
    zero = jnp.zeros((1, LANES), jnp.float32)
    at = dict(zip(places, range(len(places))))
    power = jnp.concatenate([powers[at[r]] if r in at else zero for r in range(24)], axis=0)
    along = jnp.concatenate([alongs[at[r]] if r in at else zero for r in range(24)], axis=0)
    place = lax.broadcasted_iota(jnp.int32, (24, LANES), 1)
    shift = jnp.where(place < HALF, place, place - LENGTH).astype(jnp.float32)
    total = jnp.sum(power, axis=1, keepdims=True) * 2.0**-49 + EPSILON
    by_rows = jnp.sum(along, axis=1, keepdims=True) * 2.0**-56
    by_cols = jnp.sum(power * shift, axis=1, keepdims=True) * 2.0**-49
    return by_rows / total, by_cols / total


def put_shifts(acc, step, nodes, pairs, back_ref, weigh_ref, places):
    powers, alongs = moments(pairs, back_ref, weigh_ref)
    lane = lax.broadcasted_iota(jnp.int32, (24, LANES), 1)
    each = len(places)
    for k in range(nodes):
        mine = slice(k * each, (k + 1) * each)
        by_rows, by_cols = shifts_of(powers[mine], alongs[mine], places)
        node = step * nodes + k
        here = jnp.where(lane == node, by_rows, jnp.where(lane == node + HALF, by_cols, 0.0))
        acc = acc + here
    return acc


def own_kernel(patches_ref, rows_ref, cols_ref, back_ref, weigh_ref, acc_ref, kept_ref):
    step = pl.program_id(0)
    nodes = patches_ref.shape[1]

    @pl.when(step == 0)
    def _():
        acc_ref[...] = jnp.zeros_like(acc_ref)

    spec = spectra(
        [patches_ref[s, k] for k in range(nodes) for s in range(6)], rows_ref, cols_ref
    )
    chosen = [(s, o) for o in (1, 2, 3) for s in range(6 - o)]
    pairs = []
    for k in range(nodes):
        specs = [spec[FULL * (6 * k + s) : FULL * (6 * k + s) + FULL] for s in range(6)]
        for s in range(3):
            kept_ref[k, s] = specs[3 + s]
        pairs += [cross(specs[s], specs[s + o]) for s, o in chosen]
    acc_ref[...] = put_shifts(
        acc_ref[...], step, nodes, pairs, back_ref, weigh_ref, [8 * (o - 1) + s for s, o in chosen]
    )


def next_kernel(
    tile_ref, patches_ref, kept_ref, rows_ref, cols_ref, back_ref, weigh_ref,
    own_ref, weights_ref, nodes_ref, measured_ref, message_ref,
):
    step = pl.program_id(0)
    nodes = patches_ref.shape[1]

    @pl.when(step == 0)
    def _():
        measured_ref[...] = own_ref[...]

    spec = spectra(
        [patches_ref[s, k] for k in range(nodes) for s in range(3)], rows_ref, cols_ref
    )
    chosen = [(s, o) for o in (1, 2, 3) for s in range(6 - o, 6)]
    pairs = []
    for k in range(nodes):
        ahead = [spec[FULL * (3 * k + s) : FULL * (3 * k + s) + FULL] for s in range(3)]
        pairs += [cross(kept_ref[k, s - 3], ahead[s + o - 6]) for s, o in chosen]
    measured_ref[...] = put_shifts(
        measured_ref[...], step, nodes, pairs, back_ref, weigh_ref, [8 * (o - 1) + s for s, o in chosen]
    )

    @pl.when(step == pl.num_programs(0) - 1)
    def _():
        measured = measured_ref[...] * weights_ref[...]
        measured_ref[...] = measured
        turn = tile_ref[0] * 16
        row = lax.broadcasted_iota(jnp.int32, (8, LANES), 0)
        zero = jnp.zeros((8, LANES), jnp.float32)
        low = jnp.zeros((16, LANES), jnp.float32)
        for o in (1, 2, 3):
            part = measured[8 * o - 8 : 8 * o]
            wide = jnp.concatenate([part, zero], axis=0)
            low = low - wide + pltpu.roll(wide, o, 0)
        lane = lax.broadcasted_iota(jnp.int32, (8, LANES), 1)
        flags = zero
        for o in (1, 2, 3):
            flags = jnp.where(lane == o - 1, weights_ref[8 * o - 8 : 8 * o], flags)
        message = jnp.concatenate([nodes_ref[...], flags, low], axis=0)
        message_ref[...] = pltpu.roll(message, turn, 1)


def relax_kernel(tile_ref, near_ref, low_ref, high_ref, out_ref, u_ref, w_ref, b_ref):
    u_ref[...] = jnp.zeros_like(u_ref)
    w_ref[...] = jnp.zeros_like(w_ref)
    b_ref[...] = jnp.zeros_like(b_ref)
    for trio, centre in ((low_ref, 1), (near_ref, 4), (high_ref, 7)):
        for part, by in ((0, 0), (1, -1), (2, 1)):
            row = 6 * (centre + by)
            u_ref[row : row + 6] = trio[part, 0:6]
            w_ref[row : row + 6] = trio[part, 8:14]
            b_ref[row : row + 9] += trio[part, 16:25]
    u = u_ref[...]
    flags = w_ref[...]
    lane = lax.broadcasted_iota(jnp.int32, u.shape, 1)
    weights = [
        jnp.sum(jnp.where(lane % 16 == o, flags, 0.0)[:, :HALF], axis=1, keepdims=True) * 0.25
        for o in range(3)
    ]
    weights = [jnp.broadcast_to(w, u.shape) for w in weights]
    pull = b_ref[...]
    col = lane % 8
    row = (lane // 8) % 8
    masks = [
        (m.astype(jnp.float32), by)
        for m, by in ((col > 0, 1), (col < 7, LANES - 1), (row > 0, 8), (row < 7, LANES - 8))
    ]
    degree = masks[0][0] + masks[1][0] + masks[2][0] + masks[3][0]
    for _ in range(SWEEPS):
        force = pull - degree * u
        for mask, by in masks:
            force = force + mask * pltpu.roll(u, by, 1)
        for o in (1, 2, 3):
            resid = weights[o - 1] * (pltpu.roll(u, u.shape[0] - o, 0) - u)
            force = force + resid - pltpu.roll(resid, o, 0)
        u = u + STEP_SIZE * force
    u_ref[...] = u
    turn = lax.rem(LANES - tile_ref[0] * 16, LANES)
    out_ref[...] = pltpu.roll(u_ref[24:32], turn, 1)


def shifted(value, axis, by):
    count = lax.axis_size(axis)
    pairs = [(i, i + by) for i in range(count) if 0 <= i + by < count]
    return lax.ppermute(value, axis, pairs)


def turned_by(value, axis, by):
    count = lax.axis_size(axis)
    return lax.ppermute(value, axis, [(i, (i + by) % count) for i in range(count)])


def shards(patches, pair_flags, nodes):
    local, rows_local, columns = patches.shape[:3]
    reach = pair_flags.shape[1]
    count = rows_local * columns
    flat = patches.reshape(local, count, LENGTH, LENGTH)
    tabs = tables()
    received = shifted(flat[:reach], "sec", -1)
    table_specs = [pl.BlockSpec(t.shape, lambda n: (0, 0)) for t in tabs]
    whole = pl.BlockSpec((24, LANES), lambda n: (0, 0))
    params = pltpu.CompilerParams(vmem_limit_bytes=48 * 1024 * 1024)
    own, kept = pl.pallas_call(
        own_kernel,
        grid=(count // OWN_NODES,),
        in_specs=[
            pl.BlockSpec((local, OWN_NODES, LENGTH, LENGTH), lambda n: (0, n, 0, 0)),
            *table_specs,
        ],
        out_specs=[whole, pl.BlockSpec((OWN_NODES, 3, FULL, 2 * LANES), lambda n: (n, 0, 0, 0))],
        out_shape=[
            jax.ShapeDtypeStruct((24, LANES), jnp.float32),
            jax.ShapeDtypeStruct((count, 3, FULL, 2 * LANES), jnp.bfloat16),
        ],
        compiler_params=params,
        cost_estimate=pl.CostEstimate(flops=8_000_000_000, bytes_accessed=6_000_000, transcendentals=0),
        name="own_pairs",
    )(flat, *tabs)

    sections = lax.axis_size("sec") * local
    placed = lax.axis_index("sec") * local + jnp.arange(local, dtype=jnp.int32)
    offsets = jnp.arange(1, reach + 1, dtype=jnp.int32)
    weights = pair_flags.astype(jnp.float32) * (
        placed[:, None] + offsets[None, :] < sections
    ).astype(jnp.float32)
    weight_rows = jnp.broadcast_to(
        jnp.pad(weights.T, ((0, 0), (0, 2)))[:, :, None], (reach, 8, LANES)
    ).reshape(24, LANES)
    node_rows = jnp.pad(
        jnp.transpose(nodes, (1, 0, 2, 3)).reshape(local, 2, count), ((0, 2), (0, 0), (0, HALF - count))
    ).reshape(8, LANES)
    tile = lax.axis_index("tile").astype(jnp.int32).reshape(1)

    smem = pl.BlockSpec(memory_space=pltpu.SMEM)
    measured_rows, message = pl.pallas_call(
        next_kernel,
        grid=(count // NEXT_NODES,),
        in_specs=[
            smem,
            pl.BlockSpec((reach, NEXT_NODES, LENGTH, LENGTH), lambda n: (0, n, 0, 0)),
            pl.BlockSpec((NEXT_NODES, 3, FULL, 2 * LANES), lambda n: (n, 0, 0, 0)),
            *table_specs,
            whole,
            whole,
            pl.BlockSpec((8, LANES), lambda n: (0, 0)),
        ],
        out_specs=[whole, pl.BlockSpec((32, LANES), lambda n: (0, 0))],
        out_shape=[
            jax.ShapeDtypeStruct((24, LANES), jnp.float32),
            jax.ShapeDtypeStruct((32, LANES), jnp.float32),
        ],
        compiler_params=params,
        cost_estimate=pl.CostEstimate(flops=4_000_000_000, bytes_accessed=4_000_000, transcendentals=0),
        name="next_pairs",
    )(tile, received, kept, *tabs, own, weight_rows, node_rows)

    joined = message
    for by in range(1, lax.axis_size("tile")):
        joined = joined + turned_by(message, "tile", by)
    near = jnp.stack([joined, turned_by(joined, "sec", 1), turned_by(joined, "sec", -1)], axis=0)
    low = turned_by(near, "sec", 3)
    high = turned_by(near, "sec", -3)
    relaxed_rows = pl.pallas_call(
        relax_kernel,
        in_specs=[smem] + [pl.BlockSpec(memory_space=pltpu.VMEM)] * 3,
        out_specs=pl.BlockSpec(memory_space=pltpu.VMEM),
        out_shape=jax.ShapeDtypeStruct((8, LANES), jnp.float32),
        scratch_shapes=[pltpu.VMEM((64, LANES), jnp.float32)] * 3,
        name="relax",
    )(tile, near, low, high)

    measured = jnp.transpose(
        measured_rows.reshape(reach, 8, 2, HALF)[:, :local, :, :count], (2, 1, 0, 3)
    ).reshape(2, local, reach, rows_local, columns)
    relaxed = jnp.transpose(
        relaxed_rows.reshape(8, 2, HALF)[:local, :, :count], (1, 0, 2)
    ).reshape(2, local, rows_local, columns)
    return relaxed, measured


def solution(mesh):
    placed = (P("sec", "tile", None, None, None), P("sec", None), P(None, "sec", "tile", None))
    return jax.shard_map(
        shards,
        mesh=mesh,
        in_specs=placed,
        out_specs=(P(None, "sec", "tile", None), P(None, "sec", None, "tile", None)),
        check_vma=False,
    )
```

```python
import functools

import jax
import jax.numpy as jnp
import ml_dtypes
import numpy as np
from jax import lax
from jax.experimental import pallas as pl
from jax.experimental.pallas import tpu as pltpu
from jax.sharding import PartitionSpec as P

SWEEPS = 8
STEP_SIZE = 0.08
EPSILON = 1e-06
LENGTH = 128
HALF = 64
LANES = 128
PACKS = 3
PACK_VMEM = 8
PACK_OUT = pl.BlockSpec(memory_space=pl.ANY)
OWN_VMEM = 48
BORDER_VMEM = 48
KEPT = 5
FULL = 80


def tables():
    index = np.arange(LENGTH)
    phase = (index[:, None] * index[None, :] % LENGTH) * (2.0 * np.pi / LENGTH)
    cosine, sine = np.cos(phase), np.sin(phase)
    shifts = np.where(index < HALF, index, index - LENGTH).astype(np.float64)
    rows = np.zeros((144, LENGTH))
    rows[:HALF] = cosine[:HALF]
    rows[HALF:LENGTH] = sine[:HALF]
    rows[LENGTH] = cosine[HALF]
    cols = np.block([[cosine, -sine], [-sine, -cosine]])
    back = np.block([[cosine, sine], [-sine, cosine]])
    basis = np.concatenate([2.0 * cosine[:, :HALF], -2.0 * sine[:, :HALF]], axis=1)
    basis[:, 0] = 1.0
    basis[:, HALF] = cosine[:, HALF]
    form = basis.T @ (shifts[:, None] * basis)
    cos_part = np.arange(LENGTH) <= HALF
    half_form = np.where(cos_part[None, :], form, 2.0 * form)
    weigh = np.zeros((FULL, LENGTH))
    weigh[: HALF + 1] = half_form[: HALF + 1]
    weigh = np.where(np.abs(weigh) < 1e-6, 0.0, weigh)
    top = np.zeros((144, 2 * LANES))
    top[:, :LANES] = rows
    top[:FULL, LANES:] = weigh
    return np.concatenate([top, cols, back], axis=0).astype(ml_dtypes.bfloat16)


def dot(a, b):
    return lax.dot_general(a, b, (((1,), (0,)), ((), ())), preferred_element_type=jnp.float32)


def spectra(patches, tabs_ref):
    part = dot(tabs_ref[:144, :LANES], jnp.concatenate(patches, axis=1)).astype(jnp.bfloat16)
    stacked = []
    for s in range(len(patches)):
        lanes = slice(s * LANES, (s + 1) * LANES)
        stacked.append(jnp.concatenate([part[:HALF, lanes], part[HALF:LENGTH, lanes]], axis=1))
        stacked.append(
            jnp.concatenate([part[LENGTH:, lanes], jnp.zeros((16, LANES), jnp.bfloat16)], axis=1)
        )
    return dot(jnp.concatenate(stacked, axis=0), tabs_ref[144:400]).astype(jnp.bfloat16)


def cross(a, b, sign=None):
    a = a[:72].astype(jnp.float32)
    b = b[:72].astype(jnp.float32)
    ar, ai = a[:, :LANES], a[:, LANES:]
    br, bi = b[:, :LANES], b[:, LANES:]
    real = ar * br + ai * bi
    imag = ar * bi - ai * br
    if sign is not None:
        imag = imag * sign
    top_real = real[:8] - imag[HALF:]
    top_imag = imag[:8] + real[HALF:]
    real = jnp.concatenate([top_real, real[8:HALF]], axis=0)
    imag = jnp.concatenate([top_imag, imag[8:HALF]], axis=0)
    return jnp.concatenate([real, imag], axis=1).astype(jnp.bfloat16)


def tile_sum(values):
    total = values[0:8]
    for v in range(1, HALF // 8):
        total = total + values[8 * v : 8 * v + 8]
    return total


def moments(pairs, tabs_ref):
    count = len(pairs)
    back = dot(jnp.concatenate(pairs, axis=0), tabs_ref[400:])
    reals = [back[HALF * n : HALF * n + HALF, :LANES] for n in range(count)]
    imags = [back[HALF * n : HALF * n + HALF, LANES:] for n in range(count)]
    stacked = jnp.concatenate(
        [jnp.concatenate([r, i], axis=0).astype(jnp.bfloat16) for r, i in zip(reals, imags)], axis=1
    )
    weighed = dot(tabs_ref[:FULL, LANES:], stacked)
    first = lax.broadcasted_iota(jnp.int32, (8, LANES), 0) == 0
    powers, alongs = [], []
    for n in range(count):
        real, imag = reals[n], imags[n]
        square = real * real + imag * imag
        power = 2.0 * tile_sum(square) - jnp.where(first, square[:8], 0.0)
        lanes = slice(n * LANES, (n + 1) * LANES)
        along = tile_sum(real * weighed[:HALF, lanes]) + imag[:8] * weighed[HALF:72, lanes]
        powers.append(jnp.sum(power, axis=0, keepdims=True))
        alongs.append(jnp.sum(along, axis=0, keepdims=True))
    return powers, alongs


def shifts_of(powers, alongs, places):
    zero = jnp.zeros((1, LANES), jnp.float32)
    at = dict(zip(places, range(len(places))))
    power = jnp.concatenate([powers[at[r]] if r in at else zero for r in range(24)], axis=0)
    along = jnp.concatenate([alongs[at[r]] if r in at else zero for r in range(24)], axis=0)
    place = lax.broadcasted_iota(jnp.int32, (24, LANES), 1)
    shift = jnp.where(place < HALF, place, place - LENGTH).astype(jnp.float32)
    total = jnp.sum(power, axis=1, keepdims=True) * 2.0**-49 + EPSILON
    by_rows = jnp.sum(along, axis=1, keepdims=True) * 2.0**-56
    by_cols = jnp.sum(power * shift, axis=1, keepdims=True) * 2.0**-49
    return by_rows / total, by_cols / total


def put_shifts(acc, step, nodes, pairs, tabs_ref, places):
    powers, alongs = moments(pairs, tabs_ref)
    lane = lax.broadcasted_iota(jnp.int32, (24, LANES), 1)
    each = len(places)
    for k in range(nodes):
        mine = slice(k * each, (k + 1) * each)
        by_rows, by_cols = shifts_of(powers[mine], alongs[mine], places)
        node = step * nodes + k
        here = jnp.where(lane == node, by_rows, jnp.where(lane == node + HALF, by_cols, 0.0))
        acc = acc + here
    return acc


def pack_kernel(patches_ref, first_ref, last_ref, sems):
    count = first_ref.shape[0]
    begin = patches_ref.shape[0] - count
    each = count // PACKS
    copies = []
    for n in range(2 * PACKS):
        out_ref, at = (first_ref, n * each) if n < PACKS else (last_ref, (n - PACKS) * each)
        source = at if n < PACKS else begin + at
        copies.append(
            pltpu.make_async_copy(
                patches_ref.at[pl.ds(source, each)], out_ref.at[pl.ds(at, each)], sems.at[n]
            )
        )
    for copy in copies:
        copy.start()
    for copy in copies:
        copy.wait()


def own_kernel(patches_ref, tabs_ref, acc_ref, kept_ref):
    step = pl.program_id(0)
    nodes = patches_ref.shape[1]

    @pl.when(step == 0)
    def _():
        acc_ref[...] = jnp.zeros_like(acc_ref)

    spec = spectra([patches_ref[s, k] for k in range(nodes) for s in range(6)], tabs_ref)
    chosen = [(s, o) for o in (1, 2, 3) for s in range(6 - o)]
    pairs = []
    for k in range(nodes):
        specs = [spec[FULL * (6 * k + s) : FULL * (6 * k + s) + FULL] for s in range(6)]
        for s in range(KEPT):
            kept_ref[k, s] = specs[1 + s]
        pairs += [cross(specs[s], specs[s + o]) for s, o in chosen]
    acc_ref[...] = put_shifts(
        acc_ref[...], step, nodes, pairs, tabs_ref, [8 * (o - 1) + s for s, o in chosen]
    )


def next_kernel(
    place_ref, right_ref, right_more_ref, left_ref, left_more_ref, kept_ref, tabs_ref,
    own_ref, flags_ref, nodes_ref, message_ref, acc_ref, *, sections,
):
    step = pl.program_id(0)
    nodes = right_ref.shape[0]

    @pl.when(step == 0)
    def _():
        acc_ref[...] = own_ref[...]

    early = step == 0
    sign = jnp.where(early, -1.0, 1.0).astype(jnp.float32)
    mate = jnp.where(early, 3, 0)
    inputs = []
    for k in range(nodes):
        third = jnp.where(early, right_more_ref[k], left_more_ref[k])
        inputs += [right_ref[k], left_ref[k], third]
    spec = spectra(inputs, tabs_ref)
    pairs = []
    for k in range(nodes):
        six, before, third = [spec[FULL * (3 * k + s) : FULL * (3 * k + s) + FULL] for s in range(3)]
        pairs += [cross(kept_ref[k, s - 1], six) for s in (5, 4, 3)]
        pairs += [cross(before, kept_ref[k, s - 1]) for s in (1, 2)]
        pairs.append(cross(third, kept_ref[k, mate], sign))
    acc = put_shifts(acc_ref[...], step, nodes, pairs, tabs_ref, [5, 12, 19, 14, 22, 23])
    lane = lax.broadcasted_iota(jnp.int32, (24, LANES), 1)
    row = lax.broadcasted_iota(jnp.int32, (24, LANES), 0)
    own_third = lane % HALF < nodes
    moved = pltpu.roll(acc, 21, 0)
    acc = jnp.where((row == 20) & own_third & early, moved, acc)
    acc_ref[...] = jnp.where((row == 23) & own_third, 0.0, acc)

    @pl.when(step == pl.num_programs(0) - 1)
    def _():
        gap = jnp.zeros((6, HALF - 16), jnp.float32)
        u = jnp.concatenate(
            [nodes_ref[0, :, 0], nodes_ref[0, :, 1], gap, nodes_ref[1, :, 0], nodes_ref[1, :, 1], gap],
            axis=1,
        )
        flags = jnp.concatenate(
            [flags_ref[...].astype(jnp.float32), jnp.zeros((6, LANES - 3), jnp.float32)], axis=1
        )
        ahead = place_ref[1] * 6 + lax.broadcasted_iota(jnp.int32, (6, LANES), 0)
        ahead = ahead + 1 + lax.broadcasted_iota(jnp.int32, (6, LANES), 1)
        flags = jnp.where(ahead < sections, flags, 0.0)
        two = jnp.zeros((2, LANES), jnp.float32)
        message = jnp.concatenate([u, two, flags, two, acc_ref[...]], axis=0)
        message_ref[...] = pltpu.roll(message, place_ref[0] * 16, 1)


def relax_kernel(place_ref, near_ref, low_ref, high_ref, u_out, m_out, u_ref, w_ref, m_ref):
    u_ref[...] = jnp.zeros_like(u_ref)
    w_ref[...] = jnp.zeros_like(w_ref)
    m_ref[...] = jnp.zeros_like(m_ref)
    for trio, centre in ((low_ref, 1), (near_ref, 4), (high_ref, 7)):
        for part, by in ((0, 0), (1, -1), (2, 1)):
            row = 8 + 6 * (centre + by)
            u_ref[row : row + 6] = trio[part, 0:6]
            w_ref[row : row + 6] = trio[part, 8:14]
            for o in range(3):
                m_ref[o, row : row + 6] += trio[part, 16 + 8 * o : 22 + 8 * o]
            m_ref[1, row - 1 : row] += trio[part, 30:31]
            m_ref[2, row - 1 : row] += trio[part, 38:39]
            m_ref[2, row - 2 : row - 1] += trio[part, 39:40]
    u = u_ref[...]
    flags = w_ref[...]
    lane = lax.broadcasted_iota(jnp.int32, u.shape, 1)
    pull = jnp.zeros_like(u)
    weights = []
    for o in range(3):
        weight = jnp.sum(jnp.where(lane % 16 == o, flags, 0.0), axis=1, keepdims=True) * 0.25
        weight = jnp.broadcast_to(weight, u.shape)
        weights.append(weight)
        measured = m_ref[o] * weight
        m_ref[o] = measured
        pull = pull - measured + pltpu.roll(measured, o + 1, 0)
    col = lane % 8
    row = (lane // 8) % 8
    masks = [
        (m.astype(jnp.float32), by)
        for m, by in ((col > 0, 1), (col < 7, LANES - 1), (row > 0, 8), (row < 7, LANES - 8))
    ]
    degree = masks[0][0] + masks[1][0] + masks[2][0] + masks[3][0]
    for _ in range(SWEEPS):
        force = pull - degree * u
        for mask, by in masks:
            force = force + mask * pltpu.roll(u, by, 1)
        for o in (1, 2, 3):
            resid = weights[o - 1] * (pltpu.roll(u, u.shape[0] - o, 0) - u)
            force = force + resid - pltpu.roll(resid, o, 0)
        u = u + STEP_SIZE * force
    turn = lax.rem(LANES - place_ref[0] * 16, LANES)
    relaxed = pltpu.roll(u[32:40], turn, 1)
    for c in range(2):
        for i in range(2):
            lanes = slice(HALF * c + 8 * i, HALF * c + 8 * i + 8)
            u_out[c, :, i, :] = relaxed[:6, lanes]
    for o in range(3):
        measured = pltpu.roll(m_ref[o, 32:40], turn, 1)
        for c in range(2):
            for i in range(2):
                lanes = slice(HALF * c + 8 * i, HALF * c + 8 * i + 8)
                m_out[c, :, o, i, :] = measured[:6, lanes]


def shifted(value, axis, by):
    count = lax.axis_size(axis)
    pairs = [(i, i + by) for i in range(count) if 0 <= i + by < count]
    return lax.ppermute(value, axis, pairs)


def turned_by(value, axis, by):
    count = lax.axis_size(axis)
    return lax.ppermute(value, axis, [(i, (i + by) % count) for i in range(count)])


def shards(patches, pair_flags, nodes):
    local, rows_local, columns = patches.shape[:3]
    reach = pair_flags.shape[1]
    count = rows_local * columns
    step = count // 2
    sent = count + step
    sections = lax.axis_size("sec") * local
    tabs = tables()
    own_params = pltpu.CompilerParams(vmem_limit_bytes=OWN_VMEM * 1024 * 1024)
    border_params = pltpu.CompilerParams(vmem_limit_bytes=BORDER_VMEM * 1024 * 1024)
    anywhere = pl.BlockSpec(memory_space=pl.ANY)
    smem = pl.BlockSpec(memory_space=pltpu.SMEM)
    vmem = pl.BlockSpec(memory_space=pltpu.VMEM)

    def whole(*shape):
        return pl.BlockSpec(shape, lambda n: (0,) * len(shape))

    def block(at):
        return pl.BlockSpec((step, LENGTH, LENGTH), at)

    flat = patches.reshape(local * count, LENGTH, LENGTH)
    first, last = pl.pallas_call(
        pack_kernel,
        in_specs=[pl.BlockSpec(memory_space=pltpu.HBM)],
        out_specs=[PACK_OUT] * 2,
        out_shape=[jax.ShapeDtypeStruct((sent, LENGTH, LENGTH), patches.dtype)] * 2,
        scratch_shapes=[
            pltpu.SemaphoreType.DMA((2 * PACKS,)),
        ],
        compiler_params=pltpu.CompilerParams(vmem_limit_bytes=PACK_VMEM * 1024 * 1024),
        cost_estimate=pl.CostEstimate(flops=0, bytes_accessed=3_000_000, transcendentals=0),
        name="pack",
    )(flat)
    from_right = shifted(first, "sec", -1)
    from_left = shifted(last, "sec", 1)

    own, kept = pl.pallas_call(
        own_kernel,
        grid=(count // step,),
        in_specs=[
            pl.BlockSpec((local, step, LENGTH, LENGTH), lambda n: (0, n, 0, 0)),
            whole(*tabs.shape),
        ],
        out_specs=[
            whole(24, LANES),
            pl.BlockSpec((step, KEPT, FULL, 2 * LANES), lambda n: (n, 0, 0, 0)),
        ],
        out_shape=[
            jax.ShapeDtypeStruct((24, LANES), jnp.float32),
            jax.ShapeDtypeStruct((count, KEPT, FULL, 2 * LANES), jnp.bfloat16),
        ],
        compiler_params=own_params,
        cost_estimate=pl.CostEstimate(flops=8_000_000_000, bytes_accessed=6_000_000, transcendentals=0),
        name="own_pairs",
    )(patches.reshape(local, count, LENGTH, LENGTH), tabs)

    place = jnp.stack([lax.axis_index("tile"), lax.axis_index("sec")]).astype(jnp.int32)
    message = pl.pallas_call(
        functools.partial(next_kernel, sections=sections),
        grid=(count // step,),
        in_specs=[
            smem,
            block(lambda n: (n, 0, 0)),
            block(lambda n: (2, 0, 0)),
            block(lambda n: (n + 1, 0, 0)),
            block(lambda n: (0, 0, 0)),
            pl.BlockSpec((step, KEPT, FULL, 2 * LANES), lambda n: (n, 0, 0, 0)),
            whole(*tabs.shape),
            whole(24, LANES),
            whole(*pair_flags.shape),
            whole(*nodes.shape),
        ],
        out_specs=whole(40, LANES),
        out_shape=jax.ShapeDtypeStruct((40, LANES), jnp.float32),
        scratch_shapes=[pltpu.VMEM((24, LANES), jnp.float32)],
        compiler_params=border_params,
        cost_estimate=pl.CostEstimate(flops=4_000_000_000, bytes_accessed=4_000_000, transcendentals=0),
        name="border_pairs",
    )(place, from_right, from_right, from_left, from_left, kept, tabs, own, pair_flags, nodes)

    joined = message
    for by in range(1, lax.axis_size("tile")):
        joined = joined + turned_by(message, "tile", by)
    near = jnp.stack([joined, turned_by(joined, "sec", 1), turned_by(joined, "sec", -1)], axis=0)
    low = turned_by(near, "sec", 3)
    high = turned_by(near, "sec", -3)
    return pl.pallas_call(
        relax_kernel,
        in_specs=[smem] + [vmem] * 3,
        out_specs=[vmem] * 2,
        out_shape=[
            jax.ShapeDtypeStruct(nodes.shape, jnp.float32),
            jax.ShapeDtypeStruct((2, local, reach, rows_local, columns), jnp.float32),
        ],
        scratch_shapes=[
            pltpu.VMEM((72, LANES), jnp.float32),
            pltpu.VMEM((72, LANES), jnp.float32),
            pltpu.VMEM((3, 72, LANES), jnp.float32),
        ],
        compiler_params=pltpu.CompilerParams(vmem_limit_bytes=8 * 1024 * 1024),
        name="relax",
    )(place, near, low, high)


def solution(mesh):
    placed = (P("sec", "tile", None, None, None), P("sec", None), P(None, "sec", "tile", None))
    return jax.shard_map(
        shards,
        mesh=mesh,
        in_specs=placed,
        out_specs=(P(None, "sec", "tile", None), P(None, "sec", None, "tile", None)),
        check_vma=False,
    )
```

```python
import functools

import jax
import jax.numpy as jnp
import ml_dtypes
import numpy as np
from jax import lax
from jax.experimental import pallas as pl
from jax.experimental.pallas import tpu as pltpu
from jax.sharding import PartitionSpec as P

SWEEPS = 8
STEP_SIZE = 0.08
EPSILON = 1e-06
LENGTH = 128
HALF = 64
LANES = 128
OWN_VMEM = 32
BORDER_VMEM = 32
KEPT = 5
FULL = 80


def tables():
    index = np.arange(LENGTH)
    phase = (index[:, None] * index[None, :] % LENGTH) * (2.0 * np.pi / LENGTH)
    cosine, sine = np.cos(phase), np.sin(phase)
    shifts = np.where(index < HALF, index, index - LENGTH).astype(np.float64)
    rows = np.zeros((144, LENGTH))
    rows[:HALF] = cosine[:HALF]
    rows[HALF:LENGTH] = sine[:HALF]
    rows[LENGTH] = cosine[HALF]
    cols = np.block([[cosine, -sine], [-sine, -cosine]])
    back = np.block([[cosine, sine], [-sine, cosine]])
    basis = np.concatenate([2.0 * cosine[:, :HALF], -2.0 * sine[:, :HALF]], axis=1)
    basis[:, 0] = 1.0
    basis[:, HALF] = cosine[:, HALF]
    form = basis.T @ (shifts[:, None] * basis)
    cos_part = np.arange(LENGTH) <= HALF
    half_form = np.where(cos_part[None, :], form, 2.0 * form)
    weigh = np.zeros((FULL, LENGTH))
    weigh[: HALF + 1] = half_form[: HALF + 1]
    weigh = np.where(np.abs(weigh) < 1e-6, 0.0, weigh)
    top = np.zeros((144, 2 * LANES))
    top[:, :LANES] = rows
    top[:FULL, LANES:] = weigh
    return np.concatenate([top, cols, back], axis=0).astype(ml_dtypes.bfloat16)


def dot(a, b):
    return lax.dot_general(a, b, (((1,), (0,)), ((), ())), preferred_element_type=jnp.float32)


def spectra(patches, tabs_ref):
    part = dot(tabs_ref[:144, :LANES], jnp.concatenate(patches, axis=1)).astype(jnp.bfloat16)
    stacked = []
    for s in range(len(patches)):
        lanes = slice(s * LANES, (s + 1) * LANES)
        stacked.append(jnp.concatenate([part[:HALF, lanes], part[HALF:LENGTH, lanes]], axis=1))
        stacked.append(
            jnp.concatenate([part[LENGTH:, lanes], jnp.zeros((16, LANES), jnp.bfloat16)], axis=1)
        )
    return dot(jnp.concatenate(stacked, axis=0), tabs_ref[144:400]).astype(jnp.bfloat16)


def cross(a, b, sign=None):
    a = a[:72].astype(jnp.float32)
    b = b[:72].astype(jnp.float32)
    ar, ai = a[:, :LANES], a[:, LANES:]
    br, bi = b[:, :LANES], b[:, LANES:]
    real = ar * br + ai * bi
    imag = ar * bi - ai * br
    if sign is not None:
        imag = imag * sign
    top_real = real[:8] - imag[HALF:]
    top_imag = imag[:8] + real[HALF:]
    real = jnp.concatenate([top_real, real[8:HALF]], axis=0)
    imag = jnp.concatenate([top_imag, imag[8:HALF]], axis=0)
    return jnp.concatenate([real, imag], axis=1).astype(jnp.bfloat16)


def tile_sum(values):
    total = values[0:8]
    for v in range(1, HALF // 8):
        total = total + values[8 * v : 8 * v + 8]
    return total


def moments(pairs, tabs_ref):
    count = len(pairs)
    back = dot(jnp.concatenate(pairs, axis=0), tabs_ref[400:])
    reals = [back[HALF * n : HALF * n + HALF, :LANES] for n in range(count)]
    imags = [back[HALF * n : HALF * n + HALF, LANES:] for n in range(count)]
    stacked = jnp.concatenate(
        [jnp.concatenate([r, i], axis=0).astype(jnp.bfloat16) for r, i in zip(reals, imags)], axis=1
    )
    weighed = dot(tabs_ref[:FULL, LANES:], stacked)
    first = lax.broadcasted_iota(jnp.int32, (8, LANES), 0) == 0
    powers, alongs = [], []
    for n in range(count):
        real, imag = reals[n], imags[n]
        square = real * real + imag * imag
        power = 2.0 * tile_sum(square) - jnp.where(first, square[:8], 0.0)
        lanes = slice(n * LANES, (n + 1) * LANES)
        along = tile_sum(real * weighed[:HALF, lanes]) + imag[:8] * weighed[HALF:72, lanes]
        powers.append(jnp.sum(power, axis=0, keepdims=True))
        alongs.append(jnp.sum(along, axis=0, keepdims=True))
    return powers, alongs


def shifts_of(powers, alongs, places):
    zero = jnp.zeros((1, LANES), jnp.float32)
    at = dict(zip(places, range(len(places))))
    power = jnp.concatenate([powers[at[r]] if r in at else zero for r in range(24)], axis=0)
    along = jnp.concatenate([alongs[at[r]] if r in at else zero for r in range(24)], axis=0)
    place = lax.broadcasted_iota(jnp.int32, (24, LANES), 1)
    shift = jnp.where(place < HALF, place, place - LENGTH).astype(jnp.float32)
    total = jnp.sum(power, axis=1, keepdims=True) * 2.0**-49 + EPSILON
    by_rows = jnp.sum(along, axis=1, keepdims=True) * 2.0**-56
    by_cols = jnp.sum(power * shift, axis=1, keepdims=True) * 2.0**-49
    return by_rows / total, by_cols / total


def put_shifts(acc, step, nodes, pairs, tabs_ref, places):
    powers, alongs = moments(pairs, tabs_ref)
    lane = lax.broadcasted_iota(jnp.int32, (24, LANES), 1)
    each = len(places)
    for k in range(nodes):
        mine = slice(k * each, (k + 1) * each)
        by_rows, by_cols = shifts_of(powers[mine], alongs[mine], places)
        node = step * nodes + k
        here = jnp.where(lane == node, by_rows, jnp.where(lane == node + HALF, by_cols, 0.0))
        acc = acc + here
    return acc


def pack_kernel(patches_ref, first_ref, last_ref, all_ref, sems):
    count = first_ref.shape[0]
    begin = patches_ref.shape[0] - count
    moves = [
        (patches_ref.at[pl.ds(0, count)], first_ref),
        (patches_ref.at[pl.ds(begin, count)], last_ref),
        (patches_ref, all_ref),
    ]
    copies = [pltpu.make_async_copy(*move, sems.at[n]) for n, move in enumerate(moves)]
    for copy in copies:
        copy.start()
    for copy in copies:
        copy.wait()


def own_kernel(patches_ref, tabs_ref, acc_ref, kept_ref):
    step = pl.program_id(0)
    nodes = patches_ref.shape[1]

    @pl.when(step == 0)
    def _():
        acc_ref[...] = jnp.zeros_like(acc_ref)

    spec = spectra([patches_ref[s, k] for k in range(nodes) for s in range(6)], tabs_ref)
    chosen = [(s, o) for o in (1, 2, 3) for s in range(6 - o)]
    pairs = []
    for k in range(nodes):
        specs = [spec[FULL * (6 * k + s) : FULL * (6 * k + s) + FULL] for s in range(6)]
        for s in range(KEPT):
            kept_ref[k, s] = specs[1 + s]
        pairs += [cross(specs[s], specs[s + o]) for s, o in chosen]
    acc_ref[...] = put_shifts(
        acc_ref[...], step, nodes, pairs, tabs_ref, [8 * (o - 1) + s for s, o in chosen]
    )


def next_kernel(
    place_ref, right_ref, right_more_ref, left_ref, left_more_ref, kept_ref, tabs_ref,
    own_ref, flags_ref, nodes_ref, message_ref, acc_ref, *, sections,
):
    step = pl.program_id(0)
    nodes = right_ref.shape[0]

    @pl.when(step == 0)
    def _():
        acc_ref[...] = own_ref[...]

    early = step == 0
    sign = jnp.where(early, -1.0, 1.0).astype(jnp.float32)
    mate = jnp.where(early, 3, 0)
    inputs = []
    for k in range(nodes):
        third = jnp.where(early, right_more_ref[k], left_more_ref[k])
        inputs += [right_ref[k], left_ref[k], third]
    spec = spectra(inputs, tabs_ref)
    pairs = []
    for k in range(nodes):
        six, before, third = [spec[FULL * (3 * k + s) : FULL * (3 * k + s) + FULL] for s in range(3)]
        pairs += [cross(kept_ref[k, s - 1], six) for s in (5, 4, 3)]
        pairs += [cross(before, kept_ref[k, s - 1]) for s in (1, 2)]
        pairs.append(cross(third, kept_ref[k, mate], sign))
    acc = put_shifts(acc_ref[...], step, nodes, pairs, tabs_ref, [5, 12, 19, 14, 22, 23])
    lane = lax.broadcasted_iota(jnp.int32, (24, LANES), 1)
    row = lax.broadcasted_iota(jnp.int32, (24, LANES), 0)
    own_third = lane % HALF < nodes
    moved = pltpu.roll(acc, 21, 0)
    acc = jnp.where((row == 20) & own_third & early, moved, acc)
    acc_ref[...] = jnp.where((row == 23) & own_third, 0.0, acc)

    @pl.when(step == pl.num_programs(0) - 1)
    def _():
        gap = jnp.zeros((6, HALF - 16), jnp.float32)
        u = jnp.concatenate(
            [nodes_ref[0, :, 0], nodes_ref[0, :, 1], gap, nodes_ref[1, :, 0], nodes_ref[1, :, 1], gap],
            axis=1,
        )
        given = flags_ref[...].astype(jnp.float32)
        section = lax.broadcasted_iota(jnp.int32, (6, 6), 0)
        diagonal = section == lax.broadcasted_iota(jnp.int32, (6, 6), 1)
        place = lax.broadcasted_iota(jnp.int32, (6, LANES), 1)
        flags = jnp.zeros((6, LANES), jnp.float32)
        for o in (1, 2, 3):
            wide = jnp.broadcast_to(given[o - 1 : o], (6, 6))
            column = jnp.sum(jnp.where(diagonal, wide, 0.0), axis=1, keepdims=True)
            flags = jnp.where(place == o - 1, column, flags)
        ahead = place_ref[1] * 6 + lax.broadcasted_iota(jnp.int32, (6, LANES), 0) + 1 + place
        flags = jnp.where(ahead < sections, flags, 0.0)
        two = jnp.zeros((2, LANES), jnp.float32)
        message = jnp.concatenate([u, two, flags, two, acc_ref[...]], axis=0)
        message_ref[...] = pltpu.roll(message, place_ref[0] * 16, 1)


def relax_kernel(place_ref, near_ref, low_ref, high_ref, u_out, m_out, u_ref, w_ref, m_ref):
    u_ref[...] = jnp.zeros_like(u_ref)
    w_ref[...] = jnp.zeros_like(w_ref)
    m_ref[...] = jnp.zeros_like(m_ref)
    for trio, centre in ((low_ref, 1), (near_ref, 4), (high_ref, 7)):
        for part, by in ((0, 0), (1, -1), (2, 1)):
            row = 8 + 6 * (centre + by)
            u_ref[row : row + 6] = trio[part, 0:6]
            w_ref[row : row + 6] = trio[part, 8:14]
            for o in range(3):
                m_ref[o, row : row + 6] += trio[part, 16 + 8 * o : 22 + 8 * o]
            m_ref[1, row - 1 : row] += trio[part, 30:31]
            m_ref[2, row - 1 : row] += trio[part, 38:39]
            m_ref[2, row - 2 : row - 1] += trio[part, 39:40]
    u = u_ref[...]
    flags = w_ref[...]
    lane = lax.broadcasted_iota(jnp.int32, u.shape, 1)
    pull = jnp.zeros_like(u)
    weights = []
    for o in range(3):
        weight = jnp.sum(jnp.where(lane % 16 == o, flags, 0.0), axis=1, keepdims=True) * 0.25
        weight = jnp.broadcast_to(weight, u.shape)
        weights.append(weight)
        measured = m_ref[o] * weight
        m_ref[o] = measured
        pull = pull - measured + pltpu.roll(measured, o + 1, 0)
    col = lane % 8
    row = (lane // 8) % 8
    masks = [
        (m.astype(jnp.float32), by)
        for m, by in ((col > 0, 1), (col < 7, LANES - 1), (row > 0, 8), (row < 7, LANES - 8))
    ]
    degree = masks[0][0] + masks[1][0] + masks[2][0] + masks[3][0]
    for _ in range(SWEEPS):
        force = pull - degree * u
        for mask, by in masks:
            force = force + mask * pltpu.roll(u, by, 1)
        for o in (1, 2, 3):
            resid = weights[o - 1] * (pltpu.roll(u, u.shape[0] - o, 0) - u)
            force = force + resid - pltpu.roll(resid, o, 0)
        u = u + STEP_SIZE * force
    turn = lax.rem(LANES - place_ref[0] * 16, LANES)
    relaxed = pltpu.roll(u[32:40], turn, 1)
    for c in range(2):
        for i in range(2):
            lanes = slice(HALF * c + 8 * i, HALF * c + 8 * i + 8)
            u_out[c, :, i, :] = relaxed[:6, lanes]
    for o in range(3):
        measured = pltpu.roll(m_ref[o, 32:40], turn, 1)
        for c in range(2):
            for i in range(2):
                lanes = slice(HALF * c + 8 * i, HALF * c + 8 * i + 8)
                m_out[c, :, o, i, :] = measured[:6, lanes]


def shifted(value, axis, by):
    count = lax.axis_size(axis)
    pairs = [(i, i + by) for i in range(count) if 0 <= i + by < count]
    return lax.ppermute(value, axis, pairs)


def turned_by(value, axis, by):
    count = lax.axis_size(axis)
    return lax.ppermute(value, axis, [(i, (i + by) % count) for i in range(count)])


def shards(patches, pair_flags, nodes):
    local, rows_local, columns = patches.shape[:3]
    reach = pair_flags.shape[1]
    count = rows_local * columns
    step = count // 2
    sent = count + step
    sections = lax.axis_size("sec") * local
    tabs = tables()
    own_params = pltpu.CompilerParams(vmem_limit_bytes=OWN_VMEM * 1024 * 1024)
    border_params = pltpu.CompilerParams(vmem_limit_bytes=BORDER_VMEM * 1024 * 1024)
    anywhere = pl.BlockSpec(memory_space=pl.ANY)
    smem = pl.BlockSpec(memory_space=pltpu.SMEM)
    vmem = pl.BlockSpec(memory_space=pltpu.VMEM)

    def whole(*shape):
        return pl.BlockSpec(shape, lambda n: (0,) * len(shape))

    def block(at):
        return pl.BlockSpec((step, LENGTH, LENGTH), at)

    flat = patches.reshape(local * count, LENGTH, LENGTH)
    first, last, held = pl.pallas_call(
        pack_kernel,
        in_specs=[anywhere],
        out_specs=[anywhere] * 3,
        out_shape=[
            jax.ShapeDtypeStruct((sent, LENGTH, LENGTH), patches.dtype),
            jax.ShapeDtypeStruct((sent, LENGTH, LENGTH), patches.dtype),
            jax.ShapeDtypeStruct(flat.shape, patches.dtype),
        ],
        scratch_shapes=[pltpu.SemaphoreType.DMA((4,))],
        compiler_params=pltpu.CompilerParams(vmem_limit_bytes=8 * 1024 * 1024),
        cost_estimate=pl.CostEstimate(flops=0, bytes_accessed=6_000_000, transcendentals=0),
        name="pack",
    )(flat)
    from_right = shifted(first, "sec", -1)
    from_left = shifted(last, "sec", 1)

    own, kept = pl.pallas_call(
        own_kernel,
        grid=(count // step,),
        in_specs=[
            pl.BlockSpec((local, step, LENGTH, LENGTH), lambda n: (0, n, 0, 0)),
            whole(*tabs.shape),
        ],
        out_specs=[
            whole(24, LANES),
            pl.BlockSpec((step, KEPT, FULL, 2 * LANES), lambda n: (n, 0, 0, 0)),
        ],
        out_shape=[
            jax.ShapeDtypeStruct((24, LANES), jnp.float32),
            jax.ShapeDtypeStruct((count, KEPT, FULL, 2 * LANES), jnp.bfloat16),
        ],
        compiler_params=own_params,
        cost_estimate=pl.CostEstimate(flops=8_000_000_000, bytes_accessed=6_000_000, transcendentals=0),
        name="own_pairs",
    )(held.reshape(local, count, LENGTH, LENGTH), tabs)

    place = jnp.stack([lax.axis_index("tile"), lax.axis_index("sec")]).astype(jnp.int32)
    message = pl.pallas_call(
        functools.partial(next_kernel, sections=sections),
        grid=(count // step,),
        in_specs=[
            smem,
            block(lambda n: (n, 0, 0)),
            block(lambda n: (2, 0, 0)),
            block(lambda n: (n + 1, 0, 0)),
            block(lambda n: (0, 0, 0)),
            pl.BlockSpec((step, KEPT, FULL, 2 * LANES), lambda n: (n, 0, 0, 0)),
            whole(*tabs.shape),
            whole(24, LANES),
            whole(reach, local),
            whole(*nodes.shape),
        ],
        out_specs=whole(40, LANES),
        out_shape=jax.ShapeDtypeStruct((40, LANES), jnp.float32),
        scratch_shapes=[pltpu.VMEM((24, LANES), jnp.float32)],
        compiler_params=border_params,
        cost_estimate=pl.CostEstimate(flops=4_000_000_000, bytes_accessed=4_000_000, transcendentals=0),
        name="border_pairs",
    )(place, from_right, from_right, from_left, from_left, kept, tabs, own, pair_flags.T, nodes)

    joined = message
    for by in range(1, lax.axis_size("tile")):
        joined = joined + turned_by(message, "tile", by)
    near = jnp.stack([joined, turned_by(joined, "sec", 1), turned_by(joined, "sec", -1)], axis=0)
    low = turned_by(near, "sec", 3)
    high = turned_by(near, "sec", -3)
    return pl.pallas_call(
        relax_kernel,
        in_specs=[smem] + [vmem] * 3,
        out_specs=[vmem] * 2,
        out_shape=[
            jax.ShapeDtypeStruct(nodes.shape, jnp.float32),
            jax.ShapeDtypeStruct((2, local, reach, rows_local, columns), jnp.float32),
        ],
        scratch_shapes=[
            pltpu.VMEM((72, LANES), jnp.float32),
            pltpu.VMEM((72, LANES), jnp.float32),
            pltpu.VMEM((3, 72, LANES), jnp.float32),
        ],
        compiler_params=pltpu.CompilerParams(vmem_limit_bytes=8 * 1024 * 1024),
        name="relax",
    )(place, near, low, high)


def solution(mesh):
    placed = (P("sec", "tile", None, None, None), P("sec", None), P(None, "sec", "tile", None))
    return jax.shard_map(
        shards,
        mesh=mesh,
        in_specs=placed,
        out_specs=(P(None, "sec", "tile", None), P(None, "sec", None, "tile", None)),
        check_vma=False,
    )
```

```python
import functools

import jax
import jax.numpy as jnp
import ml_dtypes
import numpy as np
from jax import lax
from jax.experimental import pallas as pl
from jax.experimental.pallas import tpu as pltpu
from jax.sharding import PartitionSpec as P

SWEEPS = 8
STEP_SIZE = 0.08
EPSILON = 1e-06
LENGTH = 128
HALF = 64
LANES = 128
OWN_VMEM = 32
BORDER_VMEM = 32
KEPT = 5
FULL = 80


def tables():
    index = np.arange(LENGTH)
    phase = (index[:, None] * index[None, :] % LENGTH) * (2.0 * np.pi / LENGTH)
    cosine, sine = np.cos(phase), np.sin(phase)
    shifts = np.where(index < HALF, index, index - LENGTH).astype(np.float64)
    rows = np.zeros((144, LENGTH))
    rows[:HALF] = cosine[:HALF]
    rows[HALF:LENGTH] = sine[:HALF]
    rows[LENGTH] = cosine[HALF]
    cols = np.block([[cosine, -sine], [-sine, -cosine]])
    back = np.block([[cosine, sine], [-sine, cosine]])
    basis = np.concatenate([2.0 * cosine[:, :HALF], -2.0 * sine[:, :HALF]], axis=1)
    basis[:, 0] = 1.0
    basis[:, HALF] = cosine[:, HALF]
    form = basis.T @ (shifts[:, None] * basis)
    cos_part = np.arange(LENGTH) <= HALF
    half_form = np.where(cos_part[None, :], form, 2.0 * form)
    weigh = np.zeros((FULL, LENGTH))
    weigh[: HALF + 1] = half_form[: HALF + 1]
    weigh = np.where(np.abs(weigh) < 1e-6, 0.0, weigh)
    top = np.zeros((144, 2 * LANES))
    top[:, :LANES] = rows
    top[:FULL, LANES:] = weigh
    return np.concatenate([top, cols, back], axis=0).astype(ml_dtypes.bfloat16)


def dot(a, b):
    return lax.dot_general(a, b, (((1,), (0,)), ((), ())), preferred_element_type=jnp.float32)


def spectra(patches, tabs_ref):
    part = dot(tabs_ref[:144, :LANES], jnp.concatenate(patches, axis=1)).astype(jnp.bfloat16)
    stacked = []
    for s in range(len(patches)):
        lanes = slice(s * LANES, (s + 1) * LANES)
        stacked.append(jnp.concatenate([part[:HALF, lanes], part[HALF:LENGTH, lanes]], axis=1))
        stacked.append(
            jnp.concatenate([part[LENGTH:, lanes], jnp.zeros((16, LANES), jnp.bfloat16)], axis=1)
        )
    return dot(jnp.concatenate(stacked, axis=0), tabs_ref[144:400]).astype(jnp.bfloat16)


def cross(a, b, sign=None):
    a = a[:72].astype(jnp.float32)
    b = b[:72].astype(jnp.float32)
    ar, ai = a[:, :LANES], a[:, LANES:]
    br, bi = b[:, :LANES], b[:, LANES:]
    real = ar * br + ai * bi
    imag = ar * bi - ai * br
    if sign is not None:
        imag = imag * sign
    top_real = real[:8] - imag[HALF:]
    top_imag = imag[:8] + real[HALF:]
    real = jnp.concatenate([top_real, real[8:HALF]], axis=0)
    imag = jnp.concatenate([top_imag, imag[8:HALF]], axis=0)
    return jnp.concatenate([real, imag], axis=1).astype(jnp.bfloat16)


def tile_sum(values):
    total = values[0:8]
    for v in range(1, HALF // 8):
        total = total + values[8 * v : 8 * v + 8]
    return total


def moments(pairs, tabs_ref):
    count = len(pairs)
    back = dot(jnp.concatenate(pairs, axis=0), tabs_ref[400:])
    reals = [back[HALF * n : HALF * n + HALF, :LANES] for n in range(count)]
    imags = [back[HALF * n : HALF * n + HALF, LANES:] for n in range(count)]
    stacked = jnp.concatenate(
        [jnp.concatenate([r, i], axis=0).astype(jnp.bfloat16) for r, i in zip(reals, imags)], axis=1
    )
    weighed = dot(tabs_ref[:FULL, LANES:], stacked)
    first = lax.broadcasted_iota(jnp.int32, (8, LANES), 0) == 0
    powers, alongs = [], []
    for n in range(count):
        real, imag = reals[n], imags[n]
        square = real * real + imag * imag
        power = 2.0 * tile_sum(square) - jnp.where(first, square[:8], 0.0)
        lanes = slice(n * LANES, (n + 1) * LANES)
        along = tile_sum(real * weighed[:HALF, lanes]) + imag[:8] * weighed[HALF:72, lanes]
        powers.append(jnp.sum(power, axis=0, keepdims=True))
        alongs.append(jnp.sum(along, axis=0, keepdims=True))
    return powers, alongs


def shifts_of(powers, alongs, places):
    zero = jnp.zeros((1, LANES), jnp.float32)
    at = dict(zip(places, range(len(places))))
    power = jnp.concatenate([powers[at[r]] if r in at else zero for r in range(24)], axis=0)
    along = jnp.concatenate([alongs[at[r]] if r in at else zero for r in range(24)], axis=0)
    place = lax.broadcasted_iota(jnp.int32, (24, LANES), 1)
    shift = jnp.where(place < HALF, place, place - LENGTH).astype(jnp.float32)
    total = jnp.sum(power, axis=1, keepdims=True) * 2.0**-49 + EPSILON
    by_rows = jnp.sum(along, axis=1, keepdims=True) * 2.0**-56
    by_cols = jnp.sum(power * shift, axis=1, keepdims=True) * 2.0**-49
    return by_rows / total, by_cols / total


def put_shifts(acc, step, nodes, pairs, tabs_ref, places):
    powers, alongs = moments(pairs, tabs_ref)
    lane = lax.broadcasted_iota(jnp.int32, (24, LANES), 1)
    each = len(places)
    for k in range(nodes):
        mine = slice(k * each, (k + 1) * each)
        by_rows, by_cols = shifts_of(powers[mine], alongs[mine], places)
        node = step * nodes + k
        here = jnp.where(lane == node, by_rows, jnp.where(lane == node + HALF, by_cols, 0.0))
        acc = acc + here
    return acc


def pack_kernel(place_ref, patches_ref, outer_ref, inner_ref, all_ref, sems):
    count = outer_ref.shape[0]
    end = patches_ref.shape[0] - count
    odd = lax.rem(place_ref[1], 2)
    moves = [
        (patches_ref.at[pl.ds(odd * end, count)], outer_ref),
        (patches_ref.at[pl.ds((1 - odd) * end, count)], inner_ref),
        (patches_ref, all_ref),
    ]
    copies = [pltpu.make_async_copy(*move, sems.at[n]) for n, move in enumerate(moves)]
    for copy in copies:
        copy.start()
    for copy in copies:
        copy.wait()


def own_kernel(patches_ref, tabs_ref, acc_ref, kept_ref):
    step = pl.program_id(0)
    nodes = patches_ref.shape[1]

    @pl.when(step == 0)
    def _():
        acc_ref[...] = jnp.zeros_like(acc_ref)

    spec = spectra([patches_ref[s, k] for k in range(nodes) for s in range(6)], tabs_ref)
    chosen = [(s, o) for o in (1, 2, 3) for s in range(6 - o)]
    pairs = []
    for k in range(nodes):
        specs = [spec[FULL * (6 * k + s) : FULL * (6 * k + s) + FULL] for s in range(6)]
        for s in range(KEPT):
            kept_ref[k, s] = specs[1 + s]
        pairs += [cross(specs[s], specs[s + o]) for s, o in chosen]
    acc_ref[...] = put_shifts(
        acc_ref[...], step, nodes, pairs, tabs_ref, [8 * (o - 1) + s for s, o in chosen]
    )


def next_kernel(
    place_ref, outer_ref, inner_ref, kept_ref, tabs_ref,
    own_ref, flags_ref, nodes_ref, message_ref, acc_ref, *, sections,
):
    step = pl.program_id(0)
    nodes = kept_ref.shape[0]
    odd = lax.rem(place_ref[1], 2) == 1

    @pl.when(step == 0)
    def _():
        acc_ref[...] = own_ref[...]

    early = step == 0
    sign = jnp.where(early, -1.0, 1.0).astype(jnp.float32)
    mate = jnp.where(early, 3, 0)
    use_outer = early == odd
    inputs = []
    for k in range(nodes):
        at = step * nodes + k
        right = jnp.where(odd, outer_ref[at], inner_ref[at])
        left = jnp.where(odd, inner_ref[at + nodes], outer_ref[at + nodes])
        more = jnp.where(early, 2 * nodes, 0) + k
        third = jnp.where(use_outer, outer_ref[more], inner_ref[more])
        inputs += [right, left, third]
    spec = spectra(inputs, tabs_ref)
    pairs = []
    for k in range(nodes):
        six, before, third = [spec[FULL * (3 * k + s) : FULL * (3 * k + s) + FULL] for s in range(3)]
        pairs += [cross(kept_ref[k, s - 1], six) for s in (5, 4, 3)]
        pairs += [cross(before, kept_ref[k, s - 1]) for s in (1, 2)]
        pairs.append(cross(third, kept_ref[k, mate], sign))
    acc = put_shifts(acc_ref[...], step, nodes, pairs, tabs_ref, [5, 12, 19, 14, 22, 23])
    lane = lax.broadcasted_iota(jnp.int32, (24, LANES), 1)
    row = lax.broadcasted_iota(jnp.int32, (24, LANES), 0)
    own_third = lane % HALF < nodes
    moved = pltpu.roll(acc, 21, 0)
    acc = jnp.where((row == 20) & own_third & early, moved, acc)
    acc_ref[...] = jnp.where((row == 23) & own_third, 0.0, acc)

    @pl.when(step == pl.num_programs(0) - 1)
    def _():
        gap = jnp.zeros((6, HALF - 16), jnp.float32)
        u = jnp.concatenate(
            [nodes_ref[0, :, 0], nodes_ref[0, :, 1], gap, nodes_ref[1, :, 0], nodes_ref[1, :, 1], gap],
            axis=1,
        )
        given = flags_ref[...].astype(jnp.float32)
        section = lax.broadcasted_iota(jnp.int32, (6, 6), 0)
        diagonal = section == lax.broadcasted_iota(jnp.int32, (6, 6), 1)
        place = lax.broadcasted_iota(jnp.int32, (6, LANES), 1)
        flags = jnp.zeros((6, LANES), jnp.float32)
        for o in (1, 2, 3):
            wide = jnp.broadcast_to(given[o - 1 : o], (6, 6))
            column = jnp.sum(jnp.where(diagonal, wide, 0.0), axis=1, keepdims=True)
            flags = jnp.where(place == o - 1, column, flags)
        ahead = place_ref[1] * 6 + lax.broadcasted_iota(jnp.int32, (6, LANES), 0) + 1 + place
        flags = jnp.where(ahead < sections, flags, 0.0)
        two = jnp.zeros((2, LANES), jnp.float32)
        message = jnp.concatenate([u, two, flags, two, acc_ref[...]], axis=0)
        message_ref[...] = pltpu.roll(message, place_ref[0] * 16, 1)


def relax_kernel(place_ref, near_ref, low_ref, high_ref, u_out, m_out, u_ref, w_ref, m_ref):
    u_ref[...] = jnp.zeros_like(u_ref)
    w_ref[...] = jnp.zeros_like(w_ref)
    m_ref[...] = jnp.zeros_like(m_ref)
    for trio, centre in ((low_ref, 1), (near_ref, 4), (high_ref, 7)):
        for part, by in ((0, 0), (1, -1), (2, 1)):
            row = 8 + 6 * (centre + by)
            u_ref[row : row + 6] = trio[part, 0:6]
            w_ref[row : row + 6] = trio[part, 8:14]
            for o in range(3):
                m_ref[o, row : row + 6] += trio[part, 16 + 8 * o : 22 + 8 * o]
            m_ref[1, row - 1 : row] += trio[part, 30:31]
            m_ref[2, row - 1 : row] += trio[part, 38:39]
            m_ref[2, row - 2 : row - 1] += trio[part, 39:40]
    u = u_ref[...]
    flags = w_ref[...]
    lane = lax.broadcasted_iota(jnp.int32, u.shape, 1)
    pull = jnp.zeros_like(u)
    weights = []
    for o in range(3):
        weight = jnp.sum(jnp.where(lane % 16 == o, flags, 0.0), axis=1, keepdims=True) * 0.25
        weight = jnp.broadcast_to(weight, u.shape)
        weights.append(weight)
        measured = m_ref[o] * weight
        m_ref[o] = measured
        pull = pull - measured + pltpu.roll(measured, o + 1, 0)
    col = lane % 8
    row = (lane // 8) % 8
    masks = [
        (m.astype(jnp.float32), by)
        for m, by in ((col > 0, 1), (col < 7, LANES - 1), (row > 0, 8), (row < 7, LANES - 8))
    ]
    degree = masks[0][0] + masks[1][0] + masks[2][0] + masks[3][0]
    for _ in range(SWEEPS):
        force = pull - degree * u
        for mask, by in masks:
            force = force + mask * pltpu.roll(u, by, 1)
        for o in (1, 2, 3):
            resid = weights[o - 1] * (pltpu.roll(u, u.shape[0] - o, 0) - u)
            force = force + resid - pltpu.roll(resid, o, 0)
        u = u + STEP_SIZE * force
    turn = lax.rem(LANES - place_ref[0] * 16, LANES)
    relaxed = pltpu.roll(u[32:40], turn, 1)
    for c in range(2):
        for i in range(2):
            lanes = slice(HALF * c + 8 * i, HALF * c + 8 * i + 8)
            u_out[c, :, i, :] = relaxed[:6, lanes]
    for o in range(3):
        measured = pltpu.roll(m_ref[o, 32:40], turn, 1)
        for c in range(2):
            for i in range(2):
                lanes = slice(HALF * c + 8 * i, HALF * c + 8 * i + 8)
                m_out[c, :, o, i, :] = measured[:6, lanes]


def swapped(value, axis, start):
    count = lax.axis_size(axis)
    pairs = []
    for i in range(start, count - 1, 2):
        pairs += [(i, i + 1), (i + 1, i)]
    return lax.ppermute(value, axis, pairs)


def turned_by(value, axis, by):
    count = lax.axis_size(axis)
    return lax.ppermute(value, axis, [(i, (i + by) % count) for i in range(count)])


def shards(patches, pair_flags, nodes):
    local, rows_local, columns = patches.shape[:3]
    reach = pair_flags.shape[1]
    count = rows_local * columns
    step = count // 2
    sent = count + step
    sections = lax.axis_size("sec") * local
    tabs = tables()
    own_params = pltpu.CompilerParams(vmem_limit_bytes=OWN_VMEM * 1024 * 1024)
    border_params = pltpu.CompilerParams(vmem_limit_bytes=BORDER_VMEM * 1024 * 1024)
    anywhere = pl.BlockSpec(memory_space=pl.ANY)
    smem = pl.BlockSpec(memory_space=pltpu.SMEM)
    vmem = pl.BlockSpec(memory_space=pltpu.VMEM)

    def whole(*shape):
        return pl.BlockSpec(shape, lambda n: (0,) * len(shape))

    flat = patches.reshape(local * count, LENGTH, LENGTH)
    place = jnp.stack([lax.axis_index("tile"), lax.axis_index("sec")]).astype(jnp.int32)
    outer, inner, held = pl.pallas_call(
        pack_kernel,
        in_specs=[smem, anywhere],
        out_specs=[anywhere] * 3,
        out_shape=[
            jax.ShapeDtypeStruct((sent, LENGTH, LENGTH), patches.dtype),
            jax.ShapeDtypeStruct((sent, LENGTH, LENGTH), patches.dtype),
            jax.ShapeDtypeStruct(flat.shape, patches.dtype),
        ],
        scratch_shapes=[pltpu.SemaphoreType.DMA((3,))],
        compiler_params=pltpu.CompilerParams(vmem_limit_bytes=8 * 1024 * 1024),
        cost_estimate=pl.CostEstimate(flops=0, bytes_accessed=6_000_000, transcendentals=0),
        name="pack",
    )(place, flat)
    outer = swapped(outer, "sec", 1)
    inner = swapped(inner, "sec", 0)

    own, kept = pl.pallas_call(
        own_kernel,
        grid=(count // step,),
        in_specs=[
            pl.BlockSpec((local, step, LENGTH, LENGTH), lambda n: (0, n, 0, 0)),
            whole(*tabs.shape),
        ],
        out_specs=[
            whole(24, LANES),
            pl.BlockSpec((step, KEPT, FULL, 2 * LANES), lambda n: (n, 0, 0, 0)),
        ],
        out_shape=[
            jax.ShapeDtypeStruct((24, LANES), jnp.float32),
            jax.ShapeDtypeStruct((count, KEPT, FULL, 2 * LANES), jnp.bfloat16),
        ],
        compiler_params=own_params,
        cost_estimate=pl.CostEstimate(flops=8_000_000_000, bytes_accessed=6_000_000, transcendentals=0),
        name="own_pairs",
    )(held.reshape(local, count, LENGTH, LENGTH), tabs)

    message = pl.pallas_call(
        functools.partial(next_kernel, sections=sections),
        grid=(count // step,),
        in_specs=[
            smem,
            vmem,
            vmem,
            pl.BlockSpec((step, KEPT, FULL, 2 * LANES), lambda n: (n, 0, 0, 0)),
            whole(*tabs.shape),
            whole(24, LANES),
            whole(reach, local),
            whole(*nodes.shape),
        ],
        out_specs=whole(40, LANES),
        out_shape=jax.ShapeDtypeStruct((40, LANES), jnp.float32),
        scratch_shapes=[pltpu.VMEM((24, LANES), jnp.float32)],
        compiler_params=border_params,
        cost_estimate=pl.CostEstimate(flops=4_000_000_000, bytes_accessed=4_000_000, transcendentals=0),
        name="border_pairs",
    )(place, outer, inner, kept, tabs, own, pair_flags.T, nodes)

    joined = message
    for by in range(1, lax.axis_size("tile")):
        joined = joined + turned_by(message, "tile", by)
    near = jnp.stack([joined, turned_by(joined, "sec", 1), turned_by(joined, "sec", -1)], axis=0)
    low = turned_by(near, "sec", 3)
    high = turned_by(near, "sec", -3)
    return pl.pallas_call(
        relax_kernel,
        in_specs=[smem] + [vmem] * 3,
        out_specs=[vmem] * 2,
        out_shape=[
            jax.ShapeDtypeStruct(nodes.shape, jnp.float32),
            jax.ShapeDtypeStruct((2, local, reach, rows_local, columns), jnp.float32),
        ],
        scratch_shapes=[
            pltpu.VMEM((72, LANES), jnp.float32),
            pltpu.VMEM((72, LANES), jnp.float32),
            pltpu.VMEM((3, 72, LANES), jnp.float32),
        ],
        compiler_params=pltpu.CompilerParams(vmem_limit_bytes=8 * 1024 * 1024),
        name="relax",
    )(place, near, low, high)


def solution(mesh):
    placed = (P("sec", "tile", None, None, None), P("sec", None), P(None, "sec", "tile", None))
    return jax.shard_map(
        shards,
        mesh=mesh,
        in_specs=placed,
        out_specs=(P(None, "sec", "tile", None), P(None, "sec", None, "tile", None)),
        check_vma=False,
    )
```
